32 devices in a mesh: groups: 2 (over y), expert: 16 (over z, x, core), head: 1.
Axes of the slice: x: 2, y: 2, z: 4, core: 2. Of those that a mesh axis runs over, the one named last changes fastest.
Arguments:
- sources: bfloat16 [4096, 1024], P(('groups', 'expert')), parts along dimension 0, may hold values from -6 to 6
- enc_gain: float32 [1024], replicated, may hold values from 0.1 to 1.9
- route_ids: int32 [4096, 2], P(('groups', 'expert')), parts along dimension 0, may hold values from 0 to 7, all different within a row; in each aligned block of 128 rows (0 to 127, 128 to 255, ...) at most 40 rows name the same one
- route_gates: float32 [4096, 2], P(('groups', 'expert')), parts along dimension 0, may hold values from 0.2 to 1
- w_in: bfloat16 [16, 1024, 2048], P('expert', None, 'head'), may hold values from -0.1875 to 0.1875
- w_out: bfloat16 [16, 2048, 1024], P('expert', 'head'), may hold values from -0.09375 to 0.09375
- targets: bfloat16 [4096, 1024], P(('groups', 'expert')), parts along dimension 0, may hold values from -6 to 6
- dec_gain: float32 [1024], replicated, may hold values from 0.1 to 1.9
- src_lengths: int32 [64], P(('groups', 'expert')), parts along dimension 0, may hold values from 16 to 64, as said below
- tgt_lengths: int32 [64], P(('groups', 'expert')), parts along dimension 0, may hold values from 16 to 64, as said below
- w_query: bfloat16 [1024, 1024], P('expert', 'head'), may hold values from -60 to 60
- w_key: bfloat16 [1024, 1024], P('expert', 'head'), may hold values from -0.1875 to 0.1875
- w_value: bfloat16 [1024, 1024], P('expert', 'head'), may hold values from -0.1875 to 0.1875
- w_attn: bfloat16 [1024, 1024], P('expert', 'head'), may hold values from -0.1875 to 0.1875
Outputs:
- memory: bfloat16 [4096, 1024], P(('groups', 'expert')), parts along dimension 0
- decoded: bfloat16 [4096, 1024], P(('groups', 'expert'), 'head'), parts along dimension 0
The draws below stay inside these ranges and needn't reach their ends.
There are 2 independent parts, one for each index of `groups`. The reference program is written for one: setup_inputs(seed, part) draws one part's arguments, and reference() takes and returns one part's arrays. A program takes and returns all parts, laid end to end along the dimension named above; an argument that names none is the same for every part. Nothing has to cross between parts.
Inputs may be any that keep to these rules, and one draw needn't show every extreme that they name: `route_ids`: in each aligned block of 128 rows no expert is named more than 40 times, a bound that some block reaches. `src_lengths`: some sentence has exactly 64 live tokens. `tgt_lengths`: some sentence has exactly 64 live tokens.
All inputs are finite; a program needn't handle non-finite values.
Results may differ from the reference program's by a relative error of at most 0.025.
Values may be sent and summed in bfloat16 or wider, within the bound.
No kernel may reach another device: no remote copies, remote signals or barrier semaphores. Data moves between devices by JAX's collectives and lax.ppermute only.
A program may use at most 64 MiB of HBM per device.

```python
import math
import jax
import jax.numpy as jnp
import numpy as np
from jax import lax

D = 1024
FF = 4096
HEADS = 16
DH = 64
EXPERTS = 8
SRC_LEN = 64
TGT_LEN = 64
SENT_DEV = 2
TOK_DEV = 128
CAP = 40
SENTS = 32
TOKENS = 2048
TGT_TOKENS = 2048
N_EXPERT = 16
N_HEAD = 1


def reach_lengths(key, longest):
    lengths = jax.random.randint(jax.random.fold_in(key, 11), (SENTS,), longest // 4, longest + 1)
    spot = jax.random.randint(jax.random.fold_in(key, 12), (), 0, SENTS)
    return jnp.where(jnp.arange(SENTS) == spot, longest, lengths).astype(jnp.int32)


def draw_src_lengths(key, part):
    return reach_lengths(jax.random.fold_in(key, 21), SRC_LEN)


def draw_tgt_lengths(key, part):
    return reach_lengths(jax.random.fold_in(key, 22), TGT_LEN)


def draw_w_query(key, part):
    base = jax.random.normal(jax.random.fold_in(key, 31), (D, D), jnp.float32)
    base = jnp.clip(base, -6.0, 6.0) * D ** (-0.5)
    return jnp.clip(base, -60.0, 60.0).astype(jnp.bfloat16)


def levels(stream_key, dims, shards, least, largest):
    level, own = 1.0, jax.random.fold_in(stream_key, 6)
    for dim, shards_of in shards:
        draws = jnp.exp(jax.random.uniform(jax.random.fold_in(own, dim), (shards_of,), jnp.float32, least / len(shards), largest / len(shards)))
        level = level * jnp.repeat(draws, dims[dim] // shards_of).reshape([-1 if axis == dim else 1 for axis in range(len(dims))])
    return level


def assign_block(stream_key, own, number, rows, amount, top, reach, slope):
    sequence = jax.random.permutation(stream_key, amount)
    crowded, ordinary = load_shares(amount, rows * top, reach, slope, True), load_shares(amount, rows * top, reach, slope, False)
    places = jnp.arange(amount)

    def named(sizes, rotation):
        used = int((sizes > 0).sum())
        fixed = max(1, used // 4)
        passed = fixed + (places - fixed + rotation * (used - fixed)) % max(1, amount - fixed)
        return jnp.zeros((amount,), jnp.int32).at[sequence[jnp.where(places < fixed, places, passed)]].set(jnp.asarray(sizes, jnp.int32))

    sizes = jnp.where(number % 4 == 0, named(crowded, number // 4), named(ordinary, number - number // 4 - 1))
    mixed = jax.random.permutation(jax.random.fold_in(own, 3), amount)
    giver, sink = mixed[0:amount // 2 * 2:2], mixed[1:amount // 2 * 2:2]
    room = jnp.minimum(sizes[giver] - 1, reach - sizes[sink]) // 2
    room = jnp.where((giver == sequence[0]) | (sink == sequence[0]) | (sizes[sink] == 0), 0, jnp.maximum(room, 0))
    passed = jax.random.randint(jax.random.fold_in(own, 4), (amount // 2,), 0, 1 << 20) % (room + 1)
    sizes = sizes.at[giver].add(-passed).at[sink].add(passed)
    labels = jnp.searchsorted(jnp.cumsum(sizes), jnp.arange(rows * top), side="right").astype(jnp.int32)
    grid = labels.reshape(top, rows).T
    grid = grid[jax.random.permutation(jax.random.fold_in(own, 1), rows)]
    rotation = jax.random.randint(jax.random.fold_in(own, 2), (rows, 1), 0, top)
    return jnp.take_along_axis(grid, (jnp.arange(top)[None, :] + rotation) % top, axis=1)


def load_shares(amount, total, reach, slope, full):
    portions = [(1 << 20) // math.isqrt(rank ** slope) + 1 for rank in range(1, amount + 1)]
    largest = reach if full else min(reach, max(-(-total // amount), total * portions[0] // sum(portions)))
    least = 1 if total - largest >= amount - 1 else 0
    holding, spare = [largest] + [least] * (amount - 1), total - largest - least * (amount - 1)
    while spare > 0:
        free = [i for i in range(1, amount) if holding[i] < largest] or [i for i in range(1, amount) if holding[i] < reach]
        pool, budget = sum([portions[i] for i in free]), spare
        for i in free:
            extra = min(reach - holding[i], max(1, budget * portions[i] // pool), spare)
            holding[i] = holding[i] + extra
            spare = spare - extra
    return np.array(holding)


def normal_values(own_key, dims, width, bound, shards=(), held_as=jnp.bfloat16):
    loudness = levels(own_key, dims, shards, -0.22, 0.18) if shards else 1.0
    result = jax.random.normal(own_key, dims, jnp.float32) * width * loudness
    return jnp.minimum(jnp.maximum(result, -bound), bound).astype(held_as)


def setup_inputs(seed: int = 0, part: int = 0) -> dict:
    arg_keys = jax.random.split(jax.random.key(seed), 15)
    part_splits = jax.random.split(jax.random.fold_in(arg_keys[14], part), 15)
    sources = normal_values(part_splits[0], (TOKENS, D), 1.0, 6.0, ((0, 16),))
    enc_gain = jnp.clip(1.0 + 0.18 * jax.random.normal(arg_keys[1], (D,), jnp.float32), 0.1, 1.9)
    route_ids_keys = jax.random.split(jax.random.fold_in(part_splits[2], 1), TOKENS // TOK_DEV)
    route_ids_turns = jax.random.permutation(jax.random.fold_in(part_splits[2], 3), TOKENS // TOK_DEV)
    route_ids = jax.vmap(lambda own, number: assign_block(jax.random.fold_in(part_splits[2], 2), own, number, TOK_DEV, EXPERTS, 2, CAP, 1))(route_ids_keys, route_ids_turns).reshape((TOKENS, 2))
    route_gates = jnp.clip(0.2 + 0.8 * jax.random.uniform(part_splits[3], (TOKENS, 2), jnp.float32) ** levels(part_splits[3], (TOKENS, 2), ((0, 16),), -0.2, 0.2), 0.2, 1.0)
    w_in = normal_values(arg_keys[4], (N_EXPERT, D, FF // 2), D ** -0.5, 0.1875, ((0, 16),))
    w_out = normal_values(arg_keys[5], (N_EXPERT, FF // 2, D), FF ** -0.5, 0.09375, ((0, 16),))
    targets = normal_values(part_splits[6], (TGT_TOKENS, D), 1.0, 6.0, ((0, 16),))
    dec_gain = jnp.clip(1.0 + 0.18 * jax.random.normal(arg_keys[7], (D,), jnp.float32), 0.1, 1.9)
    src_lengths = draw_src_lengths(jax.random.fold_in(jax.random.fold_in(arg_keys[14], part), 71), part)
    tgt_lengths = draw_tgt_lengths(jax.random.fold_in(jax.random.fold_in(arg_keys[14], part), 71), part)
    w_query = draw_w_query(jax.random.fold_in(arg_keys[14], 71), part)
    w_key = normal_values(arg_keys[11], (D, D), D ** -0.5, 0.1875, ((0, 16),))
    w_value = normal_values(arg_keys[12], (D, D), D ** -0.5, 0.1875, ((0, 16),))
    w_attn = normal_values(arg_keys[13], (D, D), D ** -0.5, 0.1875, ((0, 16),))
    return {"sources": sources, "enc_gain": enc_gain, "route_ids": route_ids, "route_gates": route_gates, "w_in": w_in, "w_out": w_out, "targets": targets, "dec_gain": dec_gain, "src_lengths": src_lengths, "tgt_lengths": tgt_lengths, "w_query": w_query, "w_key": w_key, "w_value": w_value, "w_attn": w_attn}


def layer_norm(rows, gain):
    rows = rows.astype(jnp.float32)
    mean = lax.optimization_barrier(jnp.mean(rows, axis=-1, keepdims=True))
    centered = rows - mean
    spread = lax.optimization_barrier(jnp.mean(centered * centered, axis=-1, keepdims=True))
    return centered * lax.rsqrt(spread + 1e-05) * gain.astype(jnp.float32)

def round_keep(values):
    rounded = lax.optimization_barrier(values.astype(jnp.bfloat16))
    return rounded.astype(jnp.float32)

def reference(sources, enc_gain, route_ids, route_gates, w_in, w_out, targets, dec_gain, src_lengths, tgt_lengths, w_query, w_key, w_value, w_attn):
    normed = layer_norm(sources, enc_gain).astype(jnp.bfloat16)
    blocks = route_ids.reshape(N_EXPERT, TOK_DEV * 2)
    onehot = (blocks[:, :, None] == jnp.arange(EXPERTS, dtype=jnp.int32)[None, None, :]).astype(jnp.int32)
    earlier = jnp.cumsum(onehot, axis=1) - onehot
    slots = lax.optimization_barrier(jnp.sum(earlier * onehot, axis=2)).astype(jnp.int32).reshape(TOKENS, 2)
    rows_per = N_EXPERT * CAP
    source_block = (jnp.arange(TOKENS, dtype=jnp.int32) // TOK_DEV).astype(jnp.int32)
    place = (route_ids * rows_per + source_block[:, None] * CAP + slots).astype(jnp.int32)
    buffer = jnp.zeros((EXPERTS * rows_per, D), jnp.bfloat16)
    buffer = buffer.at[place.reshape(-1)].set(jnp.repeat(normed, 2, axis=0))
    buffer = buffer.reshape(EXPERTS, rows_per, D)
    piece_width = FF // (2 * N_HEAD)

    def one_expert(index):
        rows = lax.dynamic_index_in_dim(buffer, index, 0, keepdims=False)
        total = jnp.zeros((rows_per, D), jnp.float32)
        for side in range(2):
            first = lax.dynamic_index_in_dim(w_in, 2 * index + side, 0, keepdims=False)
            second = lax.dynamic_index_in_dim(w_out, 2 * index + side, 0, keepdims=False)
            half = jnp.zeros((rows_per, D), jnp.float32)
            for piece in range(N_HEAD):
                lower = piece * piece_width
                hidden = jnp.maximum(jnp.dot(rows, first[:, lower:lower + piece_width], preferred_element_type=jnp.float32), 0.0).astype(jnp.bfloat16)
                term = jnp.dot(hidden, second[lower:lower + piece_width, :], preferred_element_type=jnp.float32)
                half = half + round_keep(term)
            total = total + round_keep(half)
        return total.astype(jnp.bfloat16)
    expert_out = lax.map(one_expert, jnp.arange(EXPERTS, dtype=jnp.int32)).reshape(EXPERTS * rows_per, D)
    first_pick = jnp.take(expert_out, place[:, 0], axis=0).astype(jnp.float32)
    second_pick = jnp.take(expert_out, place[:, 1], axis=0).astype(jnp.float32)
    moe = route_gates[:, 0:1] * first_pick + route_gates[:, 1:2] * second_pick
    memory = (sources.astype(jnp.float32) + moe).astype(jnp.bfloat16)
    tnormed = layer_norm(targets, dec_gain).astype(jnp.bfloat16)
    query = jnp.dot(tnormed, w_query, preferred_element_type=jnp.float32).astype(jnp.bfloat16)
    key = jnp.dot(memory, w_key, preferred_element_type=jnp.float32).astype(jnp.bfloat16)
    value = jnp.dot(memory, w_value, preferred_element_type=jnp.float32).astype(jnp.bfloat16)
    query_blocks = query.reshape(N_EXPERT, SENT_DEV, TGT_LEN, HEADS, DH)
    key_blocks = key.reshape(N_EXPERT, SENT_DEV, SRC_LEN, HEADS, DH)
    value_blocks = value.reshape(N_EXPERT, SENT_DEV, SRC_LEN, HEADS, DH)
    length_blocks = src_lengths.reshape(N_EXPERT, SENT_DEV)
    scale = DH ** (-0.5)

    def attend(pieces):
        queries, keys, values, lengths = pieces
        scores = jnp.einsum('sqhd,skhd->shqk', queries.astype(jnp.float32), keys.astype(jnp.float32)) * scale
        live = jnp.arange(SRC_LEN, dtype=jnp.int32)[None, :] < lengths[:, None]
        scores = jnp.where(live[:, None, None, :], scores, -1e+30)
        top = lax.optimization_barrier(jnp.max(scores, axis=-1, keepdims=True))
        raised = jnp.exp(scores - top)
        weights = (raised / lax.optimization_barrier(jnp.sum(raised, axis=-1, keepdims=True))).astype(jnp.bfloat16)
        return jnp.einsum('shqk,skhd->sqhd', weights.astype(jnp.float32), values.astype(jnp.float32)).astype(jnp.bfloat16)
    context = lax.map(attend, (query_blocks, key_blocks, value_blocks, length_blocks)).reshape(TGT_TOKENS, D)
    attn = jnp.dot(context, w_attn.T, preferred_element_type=jnp.float32)
    positions = jnp.arange(TGT_TOKENS, dtype=jnp.int32)
    owner = (positions // TGT_LEN).astype(jnp.int32)
    live_rows = (positions % TGT_LEN < jnp.take(tgt_lengths, owner)).astype(jnp.float32)
    decoded = ((targets.astype(jnp.float32) + attn) * live_rows[:, None]).astype(jnp.bfloat16)
    return (memory, decoded)
```

```python
import functools

import jax
import jax.numpy as jnp
from jax import lax
from jax.experimental import pallas as pl
from jax.experimental.pallas import tpu as pltpu
from jax.sharding import Mesh, PartitionSpec as P

DH = 64
F32, BF16 = jnp.float32, jnp.bfloat16
CHIPS = ("hi", "lo")
EXPERT = ("hi", "lo", "pair")
VMEM_LIMIT = 48 * 2**20


def layer_norm(rows, gain):
    rows = rows.astype(F32)
    mean = jnp.mean(rows, axis=-1, keepdims=True)
    centered = rows - mean
    spread = jnp.mean(centered * centered, axis=-1, keepdims=True)
    return centered * lax.rsqrt(spread + 1e-05) * gain


def places(ids, experts, capacity):
    tokens = ids.shape[0]
    lanes = -(-experts // 128) * 128
    expert = lax.broadcasted_iota(jnp.int32, (tokens, lanes), 1)
    first, second = (
        jnp.where(expert == ids[:, j : j + 1], 1.0, 0.0).astype(F32) for j in range(2)
    )
    row = lax.broadcasted_iota(jnp.int32, (tokens, tokens), 0)
    col = lax.broadcasted_iota(jnp.int32, (tokens, tokens), 1)
    before = jnp.where(col < row, 1.0, 0.0).astype(BF16)
    earlier = jnp.dot(before, (first + second).astype(BF16), preferred_element_type=F32)
    slots = (
        jnp.sum(earlier * first, axis=1, keepdims=True),
        jnp.sum((earlier + first) * second, axis=1, keepdims=True),
    )
    return [
        ids[:, j : j + 1].astype(F32) * capacity + slots[j] for j in range(2)
    ]


def prep_kernel(experts, capacity, sources, gain, ids, out):
    tokens = sources.shape[0]
    first, second = places(ids[...], experts, capacity)
    normed = layer_norm(sources[...], gain[...]).astype(BF16)
    slot = lax.broadcasted_iota(jnp.int32, (out.shape[0], tokens), 0).astype(F32)
    across = [jnp.transpose(jnp.broadcast_to(p, (tokens, tokens)))[0:1] for p in (first, second)]
    pick = jnp.where((slot == across[0]) | (slot == across[1]), 1.0, 0.0).astype(BF16)
    out[...] = jnp.dot(pick, normed, preferred_element_type=F32).astype(BF16)


def query_kernel(experts, capacity, targets, gain, ids, gates, w_q, query, high, low):
    tnormed = layer_norm(targets[...], gain[...]).astype(BF16)
    depth = tnormed.shape[1]
    weight = w_q[...].reshape(depth, -1)
    query[...] = jnp.dot(tnormed, weight, preferred_element_type=F32).astype(BF16)
    first, second = places(ids[...], experts, capacity)
    slot = lax.broadcasted_iota(jnp.int32, high.shape, 1).astype(F32)
    mix = jnp.where(slot == first, gates[:, 0:1], 0.0) + jnp.where(slot == second, gates[:, 1:2], 0.0)
    top = mix.astype(BF16)
    high[...] = top
    low[...] = (mix - top.astype(F32)).astype(BF16)


def ffn_kernel(rows, in_a, in_b, out_a, out_b, out, total):
    step = pl.program_id(0)

    @pl.when(step == 0)
    def _():
        total[...] = jnp.zeros_like(total)

    part = None
    for first, second in ((in_a, out_a), (in_b, out_b)):
        hidden = jnp.dot(rows[...], first[0], preferred_element_type=F32)
        hidden = jnp.maximum(hidden, 0.0).astype(BF16)
        term = jnp.dot(hidden, second[0], preferred_element_type=F32)
        part = term if part is None else part + term
    total[...] += part

    @pl.when(step == pl.num_programs(0) - 1)
    def _():
        out[...] = total[...].astype(BF16)


def memory_of(results, high, low, sources):
    moe = jnp.dot(high, results, preferred_element_type=F32) + jnp.dot(low, results, preferred_element_type=F32)
    return (sources.astype(F32) + moe).astype(BF16)


def attend(query, key, value, lengths, sentences):
    q_rows, k_rows = query.shape[0] // sentences, key.shape[0] // sentences
    both = 2 * DH
    lane = lax.broadcasted_iota(jnp.int32, (query.shape[0], both), 1)
    row = lax.broadcasted_iota(jnp.int32, (query.shape[0], key.shape[0]), 0)
    col = lax.broadcasted_iota(jnp.int32, (query.shape[0], key.shape[0]), 1)
    live = jnp.zeros(row.shape, jnp.bool_)
    for s in range(sentences):
        live = live | (
            (row >= s * q_rows) & (row < (s + 1) * q_rows)
            & (col >= s * k_rows) & (col < s * k_rows + jnp.minimum(lengths[s], k_rows))
        )
    live = jnp.concatenate((live, live), axis=0)
    contexts = []
    for pair in range(query.shape[1] // both):
        columns = slice(pair * both, (pair + 1) * both)
        q = query[:, columns]
        zero = jnp.zeros_like(q)
        q = jnp.concatenate((jnp.where(lane < DH, q, zero), jnp.where(lane < DH, zero, q)), axis=0)
        scores = lax.dot_general(q, key[:, columns], (((1,), (1,)), ((), ())), preferred_element_type=F32)
        scores = jnp.where(live, scores * DH ** (-0.5), -1e30)
        raised = jnp.exp(scores - jnp.max(scores, axis=-1, keepdims=True))
        weights = (raised / jnp.sum(raised, axis=-1, keepdims=True)).astype(BF16)
        mixed = jnp.dot(weights, value[:, columns], preferred_element_type=F32)
        half = query.shape[0]
        contexts.append(jnp.where(lane < DH, mixed[:half], mixed[half:]).astype(BF16))
    return jnp.concatenate(contexts, axis=1)


def tail_kernel(
    sentences, src_lengths, results, high, low, sources, query, w_k, w_v, w_o, memory, partial_out
):
    mem = memory_of(results[...], high[...], low[...], sources[...])
    memory[...] = mem
    depth = mem.shape[1]
    key = jnp.dot(mem, w_k[...].reshape(depth, -1), preferred_element_type=F32).astype(BF16)
    value = jnp.dot(mem, w_v[...].reshape(depth, -1), preferred_element_type=F32).astype(BF16)
    context = attend(query[...], key, value, src_lengths, sentences)
    partial_out[...] = lax.dot_general(
        context, w_o[...].reshape(depth, -1), (((1,), (1,)), ((), ())), preferred_element_type=F32
    ).astype(partial_out.dtype)


def live_rows(count, lengths, sentences):
    row = lax.broadcasted_iota(jnp.int32, (count, 1), 0)
    each = count // sentences
    live = jnp.zeros((count, 1), jnp.bool_)
    for s in range(sentences):
        live = live | ((row >= s * each) & (row < s * each + jnp.minimum(lengths[s], each)))
    return jnp.where(live, 1.0, 0.0)


def tail_whole_kernel(
    sentences, src_lengths, tgt_lengths, results, high, low, sources, query, targets,
    w_k, w_v, w_o, memory, decoded, attn
):
    tail_kernel(
        sentences, src_lengths, results, high, low, sources, query, w_k, w_v, w_o, memory, attn
    )
    live = live_rows(targets.shape[0], tgt_lengths, sentences)
    decoded[...] = ((targets[...].astype(F32) + attn[...]) * live).astype(BF16)


def whole(shape, dtype=BF16):
    return jax.ShapeDtypeStruct(shape, dtype)


def vmem(count):
    return [pl.BlockSpec(memory_space=pltpu.VMEM)] * count


def smem(count):
    return [pl.BlockSpec(memory_space=pltpu.SMEM)] * count


PARAMS = pltpu.CompilerParams(vmem_limit_bytes=VMEM_LIMIT)


def ffn(rows, in_a, in_b, out_a, out_b):
    depth, units = in_a.shape[1:]
    block = min(units, 256)
    count, width = rows.shape[0], out_a.shape[2]
    fixed = pl.BlockSpec((count, depth), lambda i: (0, 0))
    first = pl.BlockSpec((1, depth, block), lambda i: (0, 0, i))
    second = pl.BlockSpec((1, block, width), lambda i: (0, i, 0))
    return pl.pallas_call(
        ffn_kernel,
        grid=(units // block,),
        in_specs=[fixed, first, first, second, second],
        out_specs=pl.BlockSpec((count, width), lambda i: (0, 0)),
        out_shape=whole((count, width)),
        scratch_shapes=[pltpu.VMEM((count, width), F32)],
        compiler_params=PARAMS,
        cost_estimate=pl.CostEstimate(
            flops=8 * count * depth * units, bytes_accessed=8 * depth * units, transcendentals=0
        ),
    )(rows, in_a, in_b, out_a, out_b)


def partner(block):
    return lax.ppermute(block, "pair", [(0, 1), (1, 0)])


def weight_spec(gathered, index):
    shape = gathered.shape
    return pl.BlockSpec((shape[0], 1, *shape[2:]), lambda i: (0, index, 0, 0))


def shards(
    sources,
    enc_gain,
    route_ids,
    route_gates,
    w_in,
    w_out,
    targets,
    dec_gain,
    src_lengths,
    tgt_lengths,
    w_query,
    w_key,
    w_value,
    w_attn,
):
    tokens, width = sources.shape
    experts = lax.axis_size("hi") * lax.axis_size("lo")
    heads = lax.axis_size("head")
    capacity = 2 * ((5 * tokens + 4 * experts - 1) // (4 * experts))
    sentences = src_lengths.shape[0]
    enc_gain, dec_gain = enc_gain.reshape(1, -1), dec_gain.reshape(1, -1)

    stacked = jnp.stack((w_query, w_key, w_value, w_attn))
    gathered = lax.all_gather(stacked, EXPERT, axis=0, tiled=False)
    other_in, other_out = partner(w_in), partner(w_out)

    outgoing = pl.pallas_call(
        functools.partial(prep_kernel, experts, capacity),
        in_specs=vmem(3),
        out_specs=vmem(1)[0],
        out_shape=whole((experts * capacity, width)),
        compiler_params=PARAMS,
    )(sources, enc_gain, route_ids)
    arrived = lax.all_to_all(
        outgoing.reshape(experts, capacity, width), CHIPS, split_axis=0, concat_axis=0, tiled=True
    ).reshape(-1, width)
    half = ffn(arrived, w_in, other_in, w_out, other_out)
    if heads > 1:
        half = lax.psum(half.astype(F32), "head").astype(BF16)
    results = lax.all_to_all(
        half.reshape(experts, capacity, width), CHIPS, split_axis=0, concat_axis=0, tiled=True
    ).reshape(-1, width)

    columns = w_query.shape[1]
    query, high, low = pl.pallas_call(
        functools.partial(query_kernel, experts, capacity),
        grid=(1,),
        in_specs=vmem(4) + [weight_spec(gathered, 0)],
        out_specs=vmem(3),
        out_shape=(
            whole((targets.shape[0], columns)),
            whole((tokens, experts * capacity)),
            whole((tokens, experts * capacity)),
        ),
        compiler_params=PARAMS,
    )(targets, dec_gain, route_ids, route_gates, gathered)

    weights = [weight_spec(gathered, i) for i in (1, 2, 3)]
    if heads == 1:
        return pl.pallas_call(
            functools.partial(tail_whole_kernel, sentences),
            grid=(1,),
            in_specs=smem(2) + vmem(6) + weights,
            out_specs=vmem(2),
            out_shape=(whole(sources.shape), whole(targets.shape)),
            scratch_shapes=[pltpu.VMEM(targets.shape, F32)],
            compiler_params=PARAMS,
        )(
            src_lengths, tgt_lengths, results, high, low, sources, query, targets,
            gathered, gathered, gathered,
        )
    memory, partial_out = pl.pallas_call(
        functools.partial(tail_kernel, sentences),
        grid=(1,),
        in_specs=smem(1) + vmem(5) + weights,
        out_specs=vmem(2),
        out_shape=(whole(sources.shape), whole(targets.shape)),
        compiler_params=PARAMS,
    )(src_lengths, results, high, low, sources, query, gathered, gathered, gathered)
    attn = lax.psum_scatter(partial_out, "head", scatter_dimension=1, tiled=True).astype(F32)
    share = width // heads
    own = lax.dynamic_slice_in_dim(targets, lax.axis_index("head") * share, share, 1).astype(F32)
    each = targets.shape[0] // sentences
    positions = jnp.arange(targets.shape[0], dtype=jnp.int32)
    live = (positions % each < jnp.take(tgt_lengths, positions // each)).astype(F32)
    return memory, ((own + attn) * live[:, None]).astype(BF16)


def solution(mesh):
    groups, experts, heads = (mesh.shape[name] for name in ("groups", "expert", "head"))
    chips = experts // 2
    low = 2 if chips % 2 == 0 else 1
    fine = Mesh(
        mesh.devices.reshape(groups, chips // low, low, 2, heads),
        ("groups", "hi", "lo", "pair", "head"),
    )
    rows = ("groups", "hi", "lo", "pair")
    placed = (
        P(rows, None),
        P(),
        P(rows, None),
        P(rows, None),
        P(EXPERT, None, "head"),
        P(EXPERT, "head", None),
        P(rows, None),
        P(),
        P(rows),
        P(rows),
        P(EXPERT, "head"),
        P(EXPERT, "head"),
        P(EXPERT, "head"),
        P(EXPERT, "head"),
    )
    return jax.shard_map(
        shards,
        mesh=fine,
        in_specs=placed,
        out_specs=(P(rows, None), P(rows, "head")),
        check_vma=False,
    )
```

```python
import functools

import jax
import jax.numpy as jnp
from jax import lax
from jax.experimental import pallas as pl
from jax.experimental.pallas import tpu as pltpu
from jax.sharding import Mesh, PartitionSpec as P

DH = 64
F32, BF16 = jnp.float32, jnp.bfloat16
CHIPS = ("hi", "lo")
EXPERT = ("hi", "lo", "pair")
FFN_BLOCK = 1024


def layer_norm(rows, gain):
    rows = rows.astype(F32)
    mean = jnp.mean(rows, axis=-1, keepdims=True)
    centered = rows - mean
    spread = jnp.mean(centered * centered, axis=-1, keepdims=True)
    return centered * lax.rsqrt(spread + 1e-05) * gain


def places(ids, experts, capacity):
    tokens = ids.shape[1]
    count = -(-experts // 16) * 16
    expert = lax.broadcasted_iota(jnp.int32, (count, tokens), 0)
    first, second = (
        jnp.where(expert == ids[j : j + 1, :], 1.0, 0.0).astype(F32) for j in range(2)
    )
    row = lax.broadcasted_iota(jnp.int32, (tokens, tokens), 0)
    col = lax.broadcasted_iota(jnp.int32, (tokens, tokens), 1)
    before = jnp.where(row < col, 1.0, 0.0).astype(BF16)
    earlier = jnp.dot((first + second).astype(BF16), before, preferred_element_type=F32)
    slots = (
        jnp.sum(earlier * first, axis=0, keepdims=True),
        jnp.sum((earlier + first) * second, axis=0, keepdims=True),
    )
    return [ids[j : j + 1, :].astype(F32) * capacity + slots[j] for j in range(2)]


def dispatch(experts, capacity, sources, gain, ids, out):
    tokens = sources.shape[0]
    first, second = places(ids[...], experts, capacity)
    normed = layer_norm(sources[...], gain[...]).astype(BF16)
    slot = lax.broadcasted_iota(jnp.int32, (out.shape[0], tokens), 0).astype(F32)
    pick = jnp.where((slot == first) | (slot == second), 1.0, 0.0).astype(BF16)
    out[...] = jnp.dot(pick, normed, preferred_element_type=F32).astype(BF16)


def prep_kernel(experts, capacity, sources, gain, ids, out):
    dispatch(experts, capacity, sources, gain, ids, out)


def query_kernel(targets, gain, w_q, query):
    tnormed = layer_norm(targets[...], gain[...]).astype(BF16)
    weight = w_q[:, 0].reshape(tnormed.shape[1], -1)
    query[...] = jnp.dot(tnormed, weight, preferred_element_type=F32).astype(BF16)


def combine_matrix(experts, capacity, ids, gates, high, low):
    first, second = places(ids[...], experts, capacity)
    tokens, rows = high.shape
    slot = lax.broadcasted_iota(jnp.int32, (rows, tokens), 0).astype(F32)
    mix = jnp.where(slot == first, gates[0:1, :], 0.0) + jnp.where(slot == second, gates[1:2, :], 0.0)
    mix = jnp.transpose(mix)
    top = mix.astype(BF16)
    high[...] = top
    low[...] = (mix - top.astype(F32)).astype(BF16)


def preload_kernel(experts, capacity, fetched, choices, *refs):
    choice, refs_on = refs[fetched : fetched + choices], refs[fetched + choices :]
    ids, gates = refs_on[:2]
    outs, high, low, sems = refs_on[2:-3], refs_on[-3], refs_on[-2], refs_on[-1]
    copies = [
        pltpu.make_async_copy(refs[i], outs[i], sems.at[i]) for i in range(fetched)
    ]
    for copy in copies:
        copy.start()
    if choices:
        mine = lax.axis_index("pair") == lax.axis_index("groups")
        outs[fetched][...] = jnp.where(mine, choice[0][...], choice[1][...])
    combine_matrix(experts, capacity, ids, gates, high, low)
    for copy in copies:
        copy.wait()


def ffn_kernel(rows, others, w_in, w_out, *rest):
    for source, out in ((others, rest[-1]), (rows, rest[-2])):
        total = None
        block = min(w_in.shape[2], FFN_BLOCK)
        for n in range(0, w_in.shape[2], block):
            hidden = jnp.dot(source[...], w_in[0, :, n : n + block], preferred_element_type=F32)
            hidden = jnp.maximum(hidden, 0.0).astype(BF16)
            term = jnp.dot(hidden, w_out[0, n : n + block, :], preferred_element_type=F32)
            total = term if total is None else total + term
        out[...] = total.astype(BF16)


def memory_of(results, high, low, sources):
    moe = jnp.dot(high, results, preferred_element_type=F32) + jnp.dot(low, results, preferred_element_type=F32)
    return (sources.astype(F32) + moe).astype(BF16)


def attend(query, key, value, lengths, sentences):
    q_rows, k_rows = query.shape[0] // sentences, key.shape[0] // sentences
    both = 2 * DH
    lane = lax.broadcasted_iota(jnp.int32, (query.shape[0], both), 1)
    row = lax.broadcasted_iota(jnp.int32, (query.shape[0], key.shape[0]), 0)
    col = lax.broadcasted_iota(jnp.int32, (query.shape[0], key.shape[0]), 1)
    live = jnp.zeros(row.shape, jnp.bool_)
    for s in range(sentences):
        live = live | (
            (row >= s * q_rows) & (row < (s + 1) * q_rows)
            & (col >= s * k_rows) & (col < s * k_rows + jnp.minimum(lengths[s], k_rows))
        )
    live = jnp.concatenate((live, live), axis=0)
    contexts = []
    for pair in range(query.shape[1] // both):
        columns = slice(pair * both, (pair + 1) * both)
        q = query[:, columns]
        zero = jnp.zeros_like(q)
        q = jnp.concatenate((jnp.where(lane < DH, q, zero), jnp.where(lane < DH, zero, q)), axis=0)
        scores = lax.dot_general(q, key[:, columns], (((1,), (1,)), ((), ())), preferred_element_type=F32)
        scores = jnp.where(live, scores * DH ** (-0.5), -1e30)
        raised = jnp.exp(scores - jnp.max(scores, axis=-1, keepdims=True))
        weights = (raised / jnp.sum(raised, axis=-1, keepdims=True)).astype(BF16)
        mixed = jnp.dot(weights, value[:, columns], preferred_element_type=F32)
        half = query.shape[0]
        contexts.append(jnp.where(lane < DH, mixed[:half], mixed[half:]).astype(BF16))
    return jnp.concatenate(contexts, axis=1)


def tail_kernel(
    sentences, src_lengths, results, high, low, sources, query, gathered, memory, partial_out
):
    mem = memory_of(results[...], high[...], low[...], sources[...])
    memory[...] = mem
    depth = mem.shape[1]
    w_k, w_v, w_o = (gathered[:, i].reshape(depth, -1) for i in (1, 2, 3))
    key = jnp.dot(mem, w_k, preferred_element_type=F32).astype(BF16)
    value = jnp.dot(mem, w_v, preferred_element_type=F32).astype(BF16)
    context = attend(query[...], key, value, src_lengths, sentences)
    partial_out[...] = lax.dot_general(
        context, w_o, (((1,), (1,)), ((), ())), preferred_element_type=F32
    ).astype(partial_out.dtype)


def live_rows(count, lengths, sentences):
    row = lax.broadcasted_iota(jnp.int32, (count, 1), 0)
    each = count // sentences
    live = jnp.zeros((count, 1), jnp.bool_)
    for s in range(sentences):
        live = live | ((row >= s * each) & (row < s * each + jnp.minimum(lengths[s], each)))
    return jnp.where(live, 1.0, 0.0)


def whole(shape, dtype=BF16):
    return jax.ShapeDtypeStruct(shape, dtype)


def full(shape):
    return pl.BlockSpec(shape, lambda i: (0,) * len(shape))


SMEM = pl.BlockSpec(memory_space=pltpu.SMEM)
HERE = pl.BlockSpec(memory_space=pltpu.VMEM)
FAR = pl.BlockSpec(memory_space=pltpu.HBM)
ANY = pl.BlockSpec(memory_space=pl.ANY)
WIDE = pltpu.CompilerParams(vmem_limit_bytes=63 * 2**20)
TIGHT = pltpu.CompilerParams(vmem_limit_bytes=51 * 2**20)
NEAR = pltpu.CompilerParams(vmem_limit_bytes=24 * 2**20)


def estimate(flops, *operands):
    sizes = sum(x.size * x.dtype.itemsize for x in operands)
    return pl.CostEstimate(flops=flops, bytes_accessed=sizes, transcendentals=0)


def call(kernel, out_shape, *operands, specs=None, scratch=(), flops=0):
    specs = specs or {}
    in_specs = [specs.get(i, FAR) for i in range(len(operands))]
    far = [i for i, spec in enumerate(in_specs) if spec is FAR]
    count, single = len(operands), not isinstance(out_shape, tuple)

    def body(*refs):
        ins, rest = list(refs[:count]), refs[count:]
        held, sems = rest[-len(far) - 1 : -1], rest[-1]
        copies = [pltpu.make_async_copy(ins[i], held[n], sems.at[n]) for n, i in enumerate(far)]
        for copy in copies:
            copy.start()
        for copy in copies:
            copy.wait()
        for n, i in enumerate(far):
            ins[i] = held[n]
        kernel(*ins, *rest[: -len(far) - 1])

    moved = [pltpu.VMEM(operands[i].shape, operands[i].dtype) for i in far]
    return pl.pallas_call(
        body,
        grid=(1,),
        in_specs=in_specs,
        out_specs=full(out_shape.shape) if single else [full(o.shape) for o in out_shape],
        out_shape=out_shape,
        scratch_shapes=[*scratch, *moved, pltpu.SemaphoreType.DMA((len(far),))],
        compiler_params=WIDE,
        cost_estimate=estimate(flops, *operands),
    )(*operands)


def near(kernel, out_shape, *operands, tables=0, specs=None, out_specs=None, scratch=(), flops=0, params=None):
    specs = specs or {}
    single = not isinstance(out_shape, tuple)
    return pl.pallas_call(
        kernel,
        in_specs=[specs.get(i, SMEM if i < tables else HERE) for i in range(len(operands))],
        out_specs=out_specs or (HERE if single else [HERE] * len(out_shape)),
        out_shape=out_shape,
        scratch_shapes=list(scratch),
        compiler_params=params or NEAR,
        cost_estimate=estimate(flops, *operands),
    )(*operands)


def ffn(rows, others, w_in, w_out, ahead=()):
    shape = whole((rows.shape[0], w_out.shape[2]))
    return near(
        ffn_kernel,
        (shape, shape), rows, others, w_in, w_out, *ahead,
        specs={4 + i: ANY for i in range(len(ahead))},
        flops=8 * rows.shape[0] * w_in.shape[1] * w_in.shape[2],
    )


def partner(block):
    return lax.ppermute(block, "pair", [(0, 1), (1, 0)])


def prep_pair_kernel(experts, capacity, sources, gain, ids, *rest):
    weights, (out, own, sent) = rest[:-3], rest[-3:]
    core, half = lax.axis_index("pair"), own.shape[2]
    for block, turn in ((own, 1), (sent, 0)):
        for j, weight in enumerate(weights):
            block[j] = jnp.where(core == turn, weight[:, half:], weight[:, :half])
    dispatch(experts, capacity, sources, gain, ids, out)


def assemble(pieces, chips, index, matrix):
    hi, lo, group = (lax.axis_index(name) for name in ("hi", "lo", "groups"))
    for i, piece in enumerate(pieces):
        step, x, y = i // 4, i % 2, i % 4 // 2
        block = piece[index]
        chip = chips[hi, step] + (1 - lo if x else lo)
        start = (chip * 2 + (1 - group if y else group)) * block.shape[0]
        matrix[pl.ds(pl.multiple_of(start, block.shape[0]), block.shape[0]), :] = block


def query_pair_kernel(chips, targets, others, gain, *rest):
    pieces, (query, w_k, w_v, w_o, w_q) = rest[:-5], rest[-5:]
    for index, matrix in enumerate((w_q, w_k, w_v, w_o)):
        assemble(pieces, chips, index, matrix)
    rows = jnp.concatenate((targets[...], others[...]), axis=0)
    tnormed = layer_norm(rows, gain[...]).astype(BF16)
    query[...] = jnp.dot(tnormed, w_q[...], preferred_element_type=F32).astype(BF16)


def combine_kernel(results, high, low, sources, memory, again):
    value = memory_of(results[...], high[...], low[...], sources[...])
    memory[...] = value
    again[...] = value


def tail_pair_kernel(
    sentences, lengths, other_lengths, memory, others, query, w_k, w_v, w_o, kept, sent
):
    mem = jnp.concatenate((memory[...], others[...]), axis=0)
    key = jnp.dot(mem, w_k[...], preferred_element_type=F32).astype(BF16)
    value = jnp.dot(mem, w_v[...], preferred_element_type=F32).astype(BF16)
    count = memory.shape[0]
    t_count = query.shape[0] // 2
    for out, part, live in ((sent, 1, other_lengths), (kept, 0, lengths)):
        rows = slice(part * count, (part + 1) * count)
        context = attend(
            query[part * t_count : (part + 1) * t_count], key[rows], value[rows], live, sentences
        )
        out[...] = lax.dot_general(
            context, w_o[...], (((1,), (1,)), ((), ())), preferred_element_type=F32
        ).astype(out.dtype)


def final_kernel(sentences, tgt_lengths, targets, kept, received, decoded):
    live = live_rows(targets.shape[0], tgt_lengths, sentences)
    total = targets[...].astype(F32) + (kept[...] + received[...].astype(F32))
    decoded[...] = (total * live).astype(BF16)


def ring_order(count):
    return [*range(0, count, 2), *range(count - 1 - count % 2, 0, -2)]


DIAGONAL_BY_X = 2
AHEAD = (1, 2, 3, 4, 5, 6, 8, 12)


def swap(block, axis):
    return lax.ppermute(block, axis, [(0, 1), (1, 0)])


def ring_table(count):
    order = ring_order(count)
    return [
        [order[(order.index(hi) - step) % count] * 2 for step in range(count)] for hi in range(count)
    ]


def gather_pieces(piece):
    count = lax.axis_size("hi")
    order = ring_order(count)
    ring = [(order[i], order[(i + 1) % count]) for i in range(count)]
    pieces = []
    for step in range(count):
        if step:
            piece = lax.ppermute(piece, "hi", ring)
        along_x, along_y = swap(piece, "lo"), swap(piece, "groups")
        diagonal = swap(along_y, "lo") if step == DIAGONAL_BY_X else swap(along_x, "groups")
        pieces += [piece, along_x, along_y, diagonal]
    return pieces


def cross_attention_by_pairs(
    results, high, low, held, others, dec_gain, src_lengths, other_lengths, tgt_lengths, pieces
):
    sources, targets, targets_again = held
    width = sources.shape[1]
    t_tokens = targets.shape[0]
    sentences = src_lengths.shape[0]
    half = pieces[0].shape[2]
    chips = jnp.array(ring_table(lax.axis_size("hi")), jnp.int32)
    matrix = whole((width, half))
    query, w_k, w_v, w_o = near(
        query_pair_kernel,
        (whole((2 * t_tokens, half)), matrix, matrix, matrix),
        chips, targets, others, dec_gain, *pieces,
        tables=1,
        scratch=[pltpu.VMEM((width, half), BF16)],
    )
    memory, again = near(
        combine_kernel, (whole(sources.shape),) * 2, results, high, low, sources
    )
    kept, sent = near(
        functools.partial(tail_pair_kernel, sentences),
        (whole(targets.shape, F32), whole(targets.shape)),
        src_lengths, other_lengths, again, partner(memory), query, w_k, w_v, w_o,
        tables=2,
    )
    decoded = near(
        functools.partial(final_kernel, sentences),
        whole(targets.shape),
        tgt_lengths, targets_again, kept, partner(sent),
        tables=1,
    )
    return memory, decoded


def shards(
    sources,
    enc_gain,
    route_ids,
    route_gates,
    w_in,
    w_out,
    targets,
    dec_gain,
    src_lengths,
    tgt_lengths,
    w_query,
    w_key,
    w_value,
    w_attn,
):
    tokens, width = sources.shape
    experts = lax.axis_size("hi") * lax.axis_size("lo")
    heads = lax.axis_size("head")
    capacity = 2 * ((5 * tokens + 4 * experts - 1) // (4 * experts))
    sentences = src_lengths.shape[0]
    enc_gain, dec_gain = enc_gain.reshape(1, -1), dec_gain.reshape(1, -1)

    ids, gates = route_ids.T, route_gates.T
    by_pairs = heads == 1 and lax.axis_size("groups") == 2 and lax.axis_size("lo") == 2
    prep_args = (sources, enc_gain, ids)
    buffer = whole((experts * capacity, width))
    if by_pairs:
        shape = whole((4, w_query.shape[0], w_query.shape[1] // 2))
        outgoing, own, sent = call(
            functools.partial(prep_pair_kernel, experts, capacity),
            (buffer, shape, shape), *prep_args, w_query, w_key, w_value, w_attn,
        )
        choice = (own, partner(sent))
    else:
        outgoing = call(functools.partial(prep_kernel, experts, capacity), buffer, *prep_args)
        ahead, choice = (), ()
        stacked = jnp.stack((w_query, w_key, w_value, w_attn))
        gathered = lax.all_gather(stacked, EXPERT, axis=0, tiled=False)
    fetched = (w_in, w_out, sources, targets, targets)
    matrix = whole((tokens, experts * capacity))
    w_in, w_out, *held, high, low = near(
        functools.partial(preload_kernel, experts, capacity, len(fetched), len(choice)),
        (*(whole(x.shape) for x in fetched), *(whole(x.shape) for x in choice[:1]), matrix, matrix),
        *fetched, *choice, ids, gates,
        specs={i: FAR for i in range(len(fetched))},
        scratch=[pltpu.SemaphoreType.DMA((len(fetched),))],
        params=TIGHT,
    )
    if by_pairs:
        *held, piece = held
        pieces = gather_pieces(piece)
        others, other_lengths = partner(targets), partner(src_lengths)
        ahead = [pieces[i] for i in AHEAD] + [others, other_lengths]
    arrived = lax.all_to_all(
        outgoing.reshape(experts, capacity, width), CHIPS, split_axis=0, concat_axis=0, tiled=True
    ).reshape(-1, width)
    mine, theirs = ffn(arrived, partner(arrived), w_in, w_out, ahead)
    if heads > 1:
        mine, theirs = (lax.psum(x.astype(F32), "head").astype(BF16) for x in (mine, theirs))
    half = (mine.astype(F32) + partner(theirs).astype(F32)).astype(BF16)
    results = lax.all_to_all(
        half.reshape(experts, capacity, width), CHIPS, split_axis=0, concat_axis=0, tiled=True
    ).reshape(-1, width)

    if by_pairs:
        return cross_attention_by_pairs(
            results, high, low, held, others, dec_gain, src_lengths, other_lengths, tgt_lengths, pieces
        )
    query = call(query_kernel, whole((targets.shape[0], w_query.shape[1])), targets, dec_gain, gathered)
    memory, partial_out = call(
        functools.partial(tail_kernel, sentences),
        (whole(sources.shape), whole(targets.shape)),
        src_lengths, results, high, low, sources, query, gathered,
        specs={0: SMEM},
    )
    attn = lax.psum_scatter(partial_out, "head", scatter_dimension=1, tiled=True).astype(F32)
    share = width // heads
    own = lax.dynamic_slice_in_dim(targets, lax.axis_index("head") * share, share, 1).astype(F32)
    each = targets.shape[0] // sentences
    positions = jnp.arange(targets.shape[0], dtype=jnp.int32)
    live = (positions % each < jnp.take(tgt_lengths, positions // each)).astype(F32)
    return memory, ((own + attn) * live[:, None]).astype(BF16)


def solution(mesh):
    groups, experts, heads = (mesh.shape[name] for name in ("groups", "expert", "head"))
    chips = experts // 2
    low = 2 if chips % 2 == 0 else 1
    fine = Mesh(
        mesh.devices.reshape(groups, chips // low, low, 2, heads),
        ("groups", "hi", "lo", "pair", "head"),
    )
    rows = ("groups", "hi", "lo", "pair")
    placed = (
        P(rows, None),
        P(),
        P(rows, None),
        P(rows, None),
        P(EXPERT, None, "head"),
        P(EXPERT, "head", None),
        P(rows, None),
        P(),
        P(rows),
        P(rows),
        P(EXPERT, "head"),
        P(EXPERT, "head"),
        P(EXPERT, "head"),
        P(EXPERT, "head"),
    )
    return jax.shard_map(
        shards,
        mesh=fine,
        in_specs=placed,
        out_specs=(P(rows, None), P(rows, "head")),
        check_vma=False,
    )
```

```python
import functools

import jax
import jax.numpy as jnp
from jax import lax
from jax.experimental import pallas as pl
from jax.experimental.pallas import tpu as pltpu
from jax.sharding import Mesh, PartitionSpec as P

DH = 64
F32, BF16 = jnp.float32, jnp.bfloat16
CHIPS = ("hi", "lo")
EXPERT = ("hi", "lo", "pair")
FFN_BLOCK = 1024


def layer_norm(rows, gain):
    rows = rows.astype(F32)
    mean = jnp.mean(rows, axis=-1, keepdims=True)
    centered = rows - mean
    spread = jnp.mean(centered * centered, axis=-1, keepdims=True)
    return centered * lax.rsqrt(spread + 1e-05) * gain


def places(ids, experts, capacity):
    tokens = ids.shape[1]
    count = -(-experts // 16) * 16
    expert = lax.broadcasted_iota(jnp.int32, (count, tokens), 0)
    first, second = (
        jnp.where(expert == ids[j : j + 1, :], 1.0, 0.0).astype(F32) for j in range(2)
    )
    row = lax.broadcasted_iota(jnp.int32, (tokens, tokens), 0)
    col = lax.broadcasted_iota(jnp.int32, (tokens, tokens), 1)
    before = jnp.where(row < col, 1.0, 0.0).astype(BF16)
    earlier = jnp.dot((first + second).astype(BF16), before, preferred_element_type=F32)
    slots = (
        jnp.sum(earlier * first, axis=0, keepdims=True),
        jnp.sum((earlier + first) * second, axis=0, keepdims=True),
    )
    return [ids[j : j + 1, :].astype(F32) * capacity + slots[j] for j in range(2)]


def dispatch(experts, capacity, sources, gain, ids, out):
    tokens = sources.shape[0]
    first, second = places(ids[...], experts, capacity)
    normed = layer_norm(sources[...], gain[...]).astype(BF16)
    slot = lax.broadcasted_iota(jnp.int32, (out.shape[0], tokens), 0).astype(F32)
    pick = jnp.where((slot == first) | (slot == second), 1.0, 0.0).astype(BF16)
    out[...] = jnp.dot(pick, normed, preferred_element_type=F32).astype(BF16)


def prep_kernel(experts, capacity, sources, gain, ids, out):
    dispatch(experts, capacity, sources, gain, ids, out)


def query_kernel(targets, gain, w_q, query):
    tnormed = layer_norm(targets[...], gain[...]).astype(BF16)
    weight = w_q[:, 0].reshape(tnormed.shape[1], -1)
    query[...] = jnp.dot(tnormed, weight, preferred_element_type=F32).astype(BF16)


def combine_matrix(experts, capacity, ids, gates, high, low):
    first, second = places(ids[...], experts, capacity)
    tokens, rows = high.shape
    slot = lax.broadcasted_iota(jnp.int32, (rows, tokens), 0).astype(F32)
    mix = jnp.where(slot == first, gates[0:1, :], 0.0) + jnp.where(slot == second, gates[1:2, :], 0.0)
    mix = jnp.transpose(mix)
    top = mix.astype(BF16)
    high[...] = top
    low[...] = (mix - top.astype(F32)).astype(BF16)


def preload_kernel(experts, capacity, fetched, choices, *refs):
    choice, refs_on = refs[fetched : fetched + choices], refs[fetched + choices :]
    ids, gates = refs_on[:2]
    outs, high, low, sems = refs_on[2:-3], refs_on[-3], refs_on[-2], refs_on[-1]
    copies = [
        pltpu.make_async_copy(refs[i], outs[i], sems.at[i]) for i in range(fetched)
    ]
    for copy in copies:
        copy.start()
    if choices:
        mine = lax.axis_index("pair") == lax.axis_index("groups")
        outs[fetched][...] = jnp.where(mine, choice[0][...], choice[1][...])
    combine_matrix(experts, capacity, ids, gates, high, low)
    for copy in copies:
        copy.wait()


def ffn_kernel(ahead, rows, others, w_in, w_out, *rest):
    mine, theirs, held, sems = rest[ahead:]
    units = w_in.shape[2]
    block = min(units, FFN_BLOCK)
    copies = [
        pltpu.make_async_copy(w_out.at[0, pl.ds(n, block), :], held.at[pl.ds(n, block), :], sems.at[i])
        for i, n in enumerate(range(0, units, block))
    ]
    for copy in copies:
        copy.start()
    both = [
        [
            jnp.maximum(
                jnp.dot(source[...], w_in[0, :, n : n + block], preferred_element_type=F32), 0.0
            ).astype(BF16)
            for n in range(0, units, block)
        ]
        for source in (others, rows)
    ]
    for copy in copies:
        copy.wait()
    for hidden, out in zip(both, (theirs, mine)):
        total = None
        for i, part in enumerate(hidden):
            term = jnp.dot(part, held[i * block : (i + 1) * block, :], preferred_element_type=F32)
            total = term if total is None else total + term
        out[...] = total.astype(BF16)


def memory_of(results, high, low, sources):
    moe = jnp.dot(high, results, preferred_element_type=F32) + jnp.dot(low, results, preferred_element_type=F32)
    return (sources.astype(F32) + moe).astype(BF16)


def attend(query, key, value, lengths, sentences):
    q_rows, k_rows = query.shape[0] // sentences, key.shape[0] // sentences
    both = 2 * DH
    lane = lax.broadcasted_iota(jnp.int32, (query.shape[0], both), 1)
    row = lax.broadcasted_iota(jnp.int32, (query.shape[0], key.shape[0]), 0)
    col = lax.broadcasted_iota(jnp.int32, (query.shape[0], key.shape[0]), 1)
    live = jnp.zeros(row.shape, jnp.bool_)
    for s in range(sentences):
        live = live | (
            (row >= s * q_rows) & (row < (s + 1) * q_rows)
            & (col >= s * k_rows) & (col < s * k_rows + jnp.minimum(lengths[s], k_rows))
        )
    live = jnp.concatenate((live, live), axis=0)
    contexts = []
    for pair in range(query.shape[1] // both):
        columns = slice(pair * both, (pair + 1) * both)
        q = query[:, columns]
        zero = jnp.zeros_like(q)
        q = jnp.concatenate((jnp.where(lane < DH, q, zero), jnp.where(lane < DH, zero, q)), axis=0)
        scores = lax.dot_general(q, key[:, columns], (((1,), (1,)), ((), ())), preferred_element_type=F32)
        scores = jnp.where(live, scores * DH ** (-0.5), -1e30)
        raised = jnp.exp(scores - jnp.max(scores, axis=-1, keepdims=True))
        weights = (raised / jnp.sum(raised, axis=-1, keepdims=True)).astype(BF16)
        mixed = jnp.dot(weights, value[:, columns], preferred_element_type=F32)
        half = query.shape[0]
        contexts.append(jnp.where(lane < DH, mixed[:half], mixed[half:]).astype(BF16))
    return jnp.concatenate(contexts, axis=1)


def tail_kernel(
    sentences, src_lengths, results, high, low, sources, query, gathered, memory, partial_out
):
    mem = memory_of(results[...], high[...], low[...], sources[...])
    memory[...] = mem
    depth = mem.shape[1]
    w_k, w_v, w_o = (gathered[:, i].reshape(depth, -1) for i in (1, 2, 3))
    key = jnp.dot(mem, w_k, preferred_element_type=F32).astype(BF16)
    value = jnp.dot(mem, w_v, preferred_element_type=F32).astype(BF16)
    context = attend(query[...], key, value, src_lengths, sentences)
    partial_out[...] = lax.dot_general(
        context, w_o, (((1,), (1,)), ((), ())), preferred_element_type=F32
    ).astype(partial_out.dtype)


def live_rows(count, lengths, sentences):
    row = lax.broadcasted_iota(jnp.int32, (count, 1), 0)
    each = count // sentences
    live = jnp.zeros((count, 1), jnp.bool_)
    for s in range(sentences):
        live = live | ((row >= s * each) & (row < s * each + jnp.minimum(lengths[s], each)))
    return jnp.where(live, 1.0, 0.0)


def whole(shape, dtype=BF16):
    return jax.ShapeDtypeStruct(shape, dtype)


def full(shape):
    return pl.BlockSpec(shape, lambda i: (0,) * len(shape))


SMEM = pl.BlockSpec(memory_space=pltpu.SMEM)
HERE = pl.BlockSpec(memory_space=pltpu.VMEM)
FAR = pl.BlockSpec(memory_space=pltpu.HBM)
ANY = pl.BlockSpec(memory_space=pl.ANY)
WIDE = pltpu.CompilerParams(vmem_limit_bytes=63 * 2**20)
ROOM = pltpu.CompilerParams(vmem_limit_bytes=54 * 2**20)
TIGHT = pltpu.CompilerParams(vmem_limit_bytes=51 * 2**20)
NEAR = pltpu.CompilerParams(vmem_limit_bytes=24 * 2**20)


def estimate(flops, *operands):
    sizes = sum(x.size * x.dtype.itemsize for x in operands)
    return pl.CostEstimate(flops=flops, bytes_accessed=sizes, transcendentals=0)


def call(kernel, out_shape, *operands, specs=None, scratch=(), flops=0):
    specs = specs or {}
    in_specs = [specs.get(i, FAR) for i in range(len(operands))]
    far = [i for i, spec in enumerate(in_specs) if spec is FAR]
    count, single = len(operands), not isinstance(out_shape, tuple)

    def body(*refs):
        ins, rest = list(refs[:count]), refs[count:]
        held, sems = rest[-len(far) - 1 : -1], rest[-1]
        copies = [pltpu.make_async_copy(ins[i], held[n], sems.at[n]) for n, i in enumerate(far)]
        for copy in copies:
            copy.start()
        for copy in copies:
            copy.wait()
        for n, i in enumerate(far):
            ins[i] = held[n]
        kernel(*ins, *rest[: -len(far) - 1])

    moved = [pltpu.VMEM(operands[i].shape, operands[i].dtype) for i in far]
    return pl.pallas_call(
        body,
        grid=(1,),
        in_specs=in_specs,
        out_specs=full(out_shape.shape) if single else [full(o.shape) for o in out_shape],
        out_shape=out_shape,
        scratch_shapes=[*scratch, *moved, pltpu.SemaphoreType.DMA((len(far),))],
        compiler_params=WIDE,
        cost_estimate=estimate(flops, *operands),
    )(*operands)


def near(kernel, out_shape, *operands, tables=0, specs=None, out_specs=None, scratch=(), flops=0, params=None):
    specs = specs or {}
    single = not isinstance(out_shape, tuple)
    return pl.pallas_call(
        kernel,
        in_specs=[specs.get(i, SMEM if i < tables else HERE) for i in range(len(operands))],
        out_specs=out_specs or (HERE if single else [HERE] * len(out_shape)),
        out_shape=out_shape,
        scratch_shapes=list(scratch),
        compiler_params=params or NEAR,
        cost_estimate=estimate(flops, *operands),
    )(*operands)


def ffn(rows, others, w_in, w_out, ahead=()):
    shape = whole((rows.shape[0], w_out.shape[2]))
    units = w_in.shape[2]
    return near(
        functools.partial(ffn_kernel, len(ahead)),
        (shape, shape), rows, others, w_in, w_out, *ahead,
        specs={3: FAR, **{4 + i: ANY for i in range(len(ahead))}},
        scratch=[
            pltpu.VMEM(w_out.shape[1:], BF16),
            pltpu.SemaphoreType.DMA((units // min(units, FFN_BLOCK),)),
        ],
        flops=8 * rows.shape[0] * w_in.shape[1] * units,
        params=ROOM,
    )


def after(block, others):
    return pl.pallas_call(
        lambda *refs: None,
        in_specs=[ANY] * (1 + len(others)),
        out_specs=ANY,
        out_shape=whole(block.shape),
        input_output_aliases={0: 0},
    )(block, *others)


def partner(block):
    return lax.ppermute(block, "pair", [(0, 1), (1, 0)])


def prep_pair_kernel(experts, capacity, sources, gain, ids, *rest):
    weights, (out, own, sent) = rest[:-3], rest[-3:]
    core, half = lax.axis_index("pair"), own.shape[2]
    for block, turn in ((own, 1), (sent, 0)):
        for j, weight in enumerate(weights):
            block[j] = jnp.where(core == turn, weight[:, half:], weight[:, :half])
    dispatch(experts, capacity, sources, gain, ids, out)


def assemble(pieces, chips, index, matrix):
    hi, lo, group = (lax.axis_index(name) for name in ("hi", "lo", "groups"))
    for i, piece in enumerate(pieces):
        step, x, y = i // 4, i % 2, i % 4 // 2
        block = piece[index]
        chip = chips[hi, step] + (1 - lo if x else lo)
        start = (chip * 2 + (1 - group if y else group)) * block.shape[0]
        matrix[pl.ds(pl.multiple_of(start, block.shape[0]), block.shape[0]), :] = block


def query_pair_kernel(chips, targets, others, gain, *rest):
    pieces, (query, w_k, w_v, w_o, w_q) = rest[:-5], rest[-5:]
    for index, matrix in enumerate((w_q, w_k, w_v, w_o)):
        assemble(pieces, chips, index, matrix)
    rows = jnp.concatenate((targets[...], others[...]), axis=0)
    tnormed = layer_norm(rows, gain[...]).astype(BF16)
    query[...] = jnp.dot(tnormed, w_q[...], preferred_element_type=F32).astype(BF16)


def combine_kernel(results, high, low, sources, memory, again):
    value = memory_of(results[...], high[...], low[...], sources[...])
    memory[...] = value
    again[...] = value


def tail_pair_kernel(
    sentences, lengths, other_lengths, memory, others, query, w_k, w_v, w_o, kept, sent
):
    mem = jnp.concatenate((memory[...], others[...]), axis=0)
    key = jnp.dot(mem, w_k[...], preferred_element_type=F32).astype(BF16)
    value = jnp.dot(mem, w_v[...], preferred_element_type=F32).astype(BF16)
    count = memory.shape[0]
    t_count = query.shape[0] // 2
    for out, part, live in ((sent, 1, other_lengths), (kept, 0, lengths)):
        rows = slice(part * count, (part + 1) * count)
        context = attend(
            query[part * t_count : (part + 1) * t_count], key[rows], value[rows], live, sentences
        )
        out[...] = lax.dot_general(
            context, w_o[...], (((1,), (1,)), ((), ())), preferred_element_type=F32
        ).astype(out.dtype)


def final_kernel(sentences, tgt_lengths, targets, kept, received, decoded):
    live = live_rows(targets.shape[0], tgt_lengths, sentences)
    total = targets[...].astype(F32) + (kept[...] + received[...].astype(F32))
    decoded[...] = (total * live).astype(BF16)


def ring_order(count):
    return [*range(0, count, 2), *range(count - 1 - count % 2, 0, -2)]


DIAGONAL_BY_X = 2
AHEAD = (1, 2, 3, 4, 5, 6, 8, 12)


def swap(block, axis):
    return lax.ppermute(block, axis, [(0, 1), (1, 0)])


def ring_table(count):
    order = ring_order(count)
    return [
        [order[(order.index(hi) - step) % count] * 2 for step in range(count)] for hi in range(count)
    ]


def gather_pieces(piece):
    count = lax.axis_size("hi")
    order = ring_order(count)
    ring = [(order[i], order[(i + 1) % count]) for i in range(count)]
    pieces = []
    for step in range(count):
        if step:
            piece = lax.ppermute(piece, "hi", ring)
        along_x, along_y = swap(piece, "lo"), swap(piece, "groups")
        diagonal = swap(along_y, "lo") if step == DIAGONAL_BY_X else swap(along_x, "groups")
        pieces += [piece, along_x, along_y, diagonal]
    return pieces


def cross_attention_by_pairs(
    results, high, low, held, others, dec_gain, src_lengths, other_lengths, tgt_lengths, pieces
):
    sources, targets, targets_again = held
    width = sources.shape[1]
    t_tokens = targets.shape[0]
    sentences = src_lengths.shape[0]
    half = pieces[0].shape[2]
    chips = jnp.array(ring_table(lax.axis_size("hi")), jnp.int32)
    matrix = whole((width, half))
    query, w_k, w_v, w_o = near(
        query_pair_kernel,
        (whole((2 * t_tokens, half)), matrix, matrix, matrix),
        chips, targets, others, dec_gain, *pieces,
        tables=1,
        scratch=[pltpu.VMEM((width, half), BF16)],
    )
    memory, again = near(
        combine_kernel, (whole(sources.shape),) * 2, results, high, low, sources
    )
    kept, sent = near(
        functools.partial(tail_pair_kernel, sentences),
        (whole(targets.shape, F32), whole(targets.shape)),
        src_lengths, other_lengths, again, partner(memory), query, w_k, w_v, w_o,
        tables=2,
    )
    decoded = near(
        functools.partial(final_kernel, sentences),
        whole(targets.shape),
        tgt_lengths, targets_again, kept, partner(sent),
        tables=1,
    )
    return memory, decoded


def shards(
    sources,
    enc_gain,
    route_ids,
    route_gates,
    w_in,
    w_out,
    targets,
    dec_gain,
    src_lengths,
    tgt_lengths,
    w_query,
    w_key,
    w_value,
    w_attn,
):
    tokens, width = sources.shape
    experts = lax.axis_size("hi") * lax.axis_size("lo")
    heads = lax.axis_size("head")
    capacity = 2 * ((5 * tokens + 4 * experts - 1) // (4 * experts))
    sentences = src_lengths.shape[0]
    enc_gain, dec_gain = enc_gain.reshape(1, -1), dec_gain.reshape(1, -1)

    ids, gates = route_ids.T, route_gates.T
    by_pairs = heads == 1 and lax.axis_size("groups") == 2 and lax.axis_size("lo") == 2
    prep_args = (sources, enc_gain, ids)
    buffer = whole((experts * capacity, width))
    if by_pairs:
        shape = whole((4, w_query.shape[0], w_query.shape[1] // 2))
        outgoing, own, sent = call(
            functools.partial(prep_pair_kernel, experts, capacity),
            (buffer, shape, shape), *prep_args, w_query, w_key, w_value, w_attn,
        )
        choice = (own, partner(sent))
    else:
        outgoing = call(functools.partial(prep_kernel, experts, capacity), buffer, *prep_args)
        ahead, choice = (), ()
        stacked = jnp.stack((w_query, w_key, w_value, w_attn))
        gathered = lax.all_gather(stacked, EXPERT, axis=0, tiled=False)
    arrived = lax.all_to_all(
        outgoing.reshape(experts, capacity, width), CHIPS, split_axis=0, concat_axis=0, tiled=True
    ).reshape(-1, width)
    fetched = (w_in, sources, targets, targets)
    matrix = whole((tokens, experts * capacity))
    w_in, *held, high, low = near(
        functools.partial(preload_kernel, experts, capacity, len(fetched), len(choice)),
        (*(whole(x.shape) for x in fetched), *(whole(x.shape) for x in choice[:1]), matrix, matrix),
        *fetched, *choice, ids, gates,
        specs={i: FAR for i in range(len(fetched))},
        scratch=[pltpu.SemaphoreType.DMA((len(fetched),))],
        params=TIGHT,
    )
    if by_pairs:
        *held, piece = held
        pieces = gather_pieces(after(piece, [arrived]))
        others, other_lengths = partner(targets), partner(src_lengths)
        ahead = [pieces[i] for i in AHEAD] + [others, other_lengths]
    mine, theirs = ffn(arrived, partner(arrived), w_in, w_out, ahead)
    if heads > 1:
        mine, theirs = (lax.psum(x.astype(F32), "head").astype(BF16) for x in (mine, theirs))
    half = (mine.astype(F32) + partner(theirs).astype(F32)).astype(BF16)
    results = lax.all_to_all(
        half.reshape(experts, capacity, width), CHIPS, split_axis=0, concat_axis=0, tiled=True
    ).reshape(-1, width)

    if by_pairs:
        return cross_attention_by_pairs(
            results, high, low, held, others, dec_gain, src_lengths, other_lengths, tgt_lengths, pieces
        )
    query = call(query_kernel, whole((targets.shape[0], w_query.shape[1])), targets, dec_gain, gathered)
    memory, partial_out = call(
        functools.partial(tail_kernel, sentences),
        (whole(sources.shape), whole(targets.shape)),
        src_lengths, results, high, low, sources, query, gathered,
        specs={0: SMEM},
    )
    attn = lax.psum_scatter(partial_out, "head", scatter_dimension=1, tiled=True).astype(F32)
    share = width // heads
    own = lax.dynamic_slice_in_dim(targets, lax.axis_index("head") * share, share, 1).astype(F32)
    each = targets.shape[0] // sentences
    positions = jnp.arange(targets.shape[0], dtype=jnp.int32)
    live = (positions % each < jnp.take(tgt_lengths, positions // each)).astype(F32)
    return memory, ((own + attn) * live[:, None]).astype(BF16)


def solution(mesh):
    groups, experts, heads = (mesh.shape[name] for name in ("groups", "expert", "head"))
    chips = experts // 2
    low = 2 if chips % 2 == 0 else 1
    fine = Mesh(
        mesh.devices.reshape(groups, chips // low, low, 2, heads),
        ("groups", "hi", "lo", "pair", "head"),
    )
    rows = ("groups", "hi", "lo", "pair")
    placed = (
        P(rows, None),
        P(),
        P(rows, None),
        P(rows, None),
        P(EXPERT, None, "head"),
        P(EXPERT, "head", None),
        P(rows, None),
        P(),
        P(rows),
        P(rows),
        P(EXPERT, "head"),
        P(EXPERT, "head"),
        P(EXPERT, "head"),
        P(EXPERT, "head"),
    )
    return jax.shard_map(
        shards,
        mesh=fine,
        in_specs=placed,
        out_specs=(P(rows, None), P(rows, "head")),
        check_vma=False,
    )
```
